32 devices in a mesh: dp: 8 (over y, x, core), tensor: 4 (over z).
Axes of the slice: x: 2, y: 2, z: 4, core: 2. Of those that a mesh axis runs over, the one named last changes fastest.
Arguments:
- inputs: bfloat16 [8192, 2048], P(('dp', 'tensor')), may hold values from -6 to 6
- norm1_gain: float32 [2048], replicated, may hold values from 0.5 to 1.5
- query_weight: bfloat16 [2048, 1024], P('dp', 'tensor'), may hold values from -0.125 to 0.125
- key_weight: bfloat16 [2048, 1024], P('dp', 'tensor'), may hold values from -0.125 to 0.125
- value_weight: bfloat16 [2048, 2048], P('dp', 'tensor'), may hold values from -0.125 to 0.125
- outgate_weight: bfloat16 [2048, 2048], P('dp', 'tensor'), may hold values from -0.125 to 0.125
- gate_down: bfloat16 [2048, 16], replicated, may hold values from -0.125 to 0.125
- gate_up: float32 [16, 1024], P(None, 'tensor'), may hold values from -1.5 to 1.5
- gate_bias: float32 [1024], P('tensor'), may hold values from 0.5 to 4.5
- group_gain: float32 [2048], P('tensor'), may hold values from 0.5 to 1.5
- proj_weight: bfloat16 [2048, 2048], P('tensor', 'dp'), may hold values from -0.25 to 0.25
- norm2_gain: float32 [2048], replicated, may hold values from 0.5 to 1.5
- ffn_gate: bfloat16 [2048, 5632], P('dp', 'tensor'), may hold values from -0.125 to 0.125
- ffn_up: bfloat16 [2048, 5632], P('dp', 'tensor'), may hold values from -0.125 to 0.125
- ffn_down: bfloat16 [5632, 2048], P('tensor', 'dp'), may hold values from -0.109375 to 0.109375
- cotangent: bfloat16 [8192, 2048], P(('dp', 'tensor')), may hold values from -6 to 6
Outputs:
- output: bfloat16 [8192, 2048], P(('dp', 'tensor'))
- grad_input: float32 [8192, 2048], P(('dp', 'tensor'))
- grad_norm1: float32 [2048], replicated
- grad_query: float32 [2048, 1024], P('dp', 'tensor')
- grad_key: float32 [2048, 1024], P('dp', 'tensor')
- grad_value: float32 [2048, 2048], P('dp', 'tensor')
- grad_outgate: float32 [2048, 2048], P('dp', 'tensor')
- grad_gate_down: float32 [2048, 16], replicated
- grad_gate_up: float32 [16, 1024], P(None, 'tensor')
- grad_gate_bias: float32 [1024], P('tensor')
- grad_group_gain: float32 [2048], P('tensor')
- grad_proj: float32 [2048, 2048], P('tensor', 'dp')
- grad_norm2: float32 [2048], replicated
- grad_ffn_gate: float32 [2048, 5632], P('dp', 'tensor')
- grad_ffn_up: float32 [2048, 5632], P('dp', 'tensor')
- grad_ffn_down: float32 [5632, 2048], P('tensor', 'dp')
The draws below stay inside these ranges and needn't reach their ends.
All inputs are finite; a program needn't handle non-finite values.
Results may differ from the reference program's by a relative error of at most 0.025.
Values may be sent and summed in bfloat16 or wider, within the bound.
No kernel may reach another device: no remote copies, remote signals or barrier semaphores. Data moves between devices by JAX's collectives and lax.ppermute only.
A program may use at most 192 MiB of HBM per device.

```python
import jax
import jax.numpy as jnp
from jax import lax

D = 2048
HEADS = 4
KD = 1024
VD = 2048
FF = 5632
RANK = 16
BLOCK = 64
LEN = 1024
TOKENS = 8192


def shard_levels(own_key, dims, shards, smallest, high):
    def one(position, blocks):
        draws = jax.random.uniform(jax.random.fold_in(jax.random.fold_in(own_key, 6), position), (blocks,), jnp.float32, smallest / len(shards), high / len(shards))
        return jnp.repeat(jnp.exp(draws), dims[position] // blocks).reshape((-1,) + (1,) * (len(dims) - position - 1))

    level = one(*shards[0])
    for cut in shards[1:]:
        level = level * one(*cut)
    return level


def gaussian(key, dims, scale, reach, cuts=(), held_as=jnp.bfloat16):
    values = scale * jax.random.normal(key, dims, jnp.float32)
    if cuts:
        values = values * shard_levels(key, dims, cuts, -0.22, 0.18)
    return jnp.clip(values, -reach, reach).astype(held_as)


def setup_inputs(seed: int = 0) -> dict:
    arg_keys = jax.random.split(jax.random.key(seed), 17)
    return {
        "inputs": gaussian(arg_keys[0], (TOKENS, D), 1.0, 6.0, ((0, 32),)),
        "norm1_gain": jnp.clip(1.0 + 0.1 * jax.random.normal(arg_keys[1], (D,), jnp.float32), 0.5, 1.5),
        "query_weight": gaussian(arg_keys[2], (D, KD), D ** -0.5, 0.125, ((0, 8), (1, 4))),
        "key_weight": gaussian(arg_keys[3], (D, KD), D ** -0.5, 0.125, ((0, 8), (1, 4))),
        "value_weight": gaussian(arg_keys[4], (D, VD), D ** -0.5, 0.125, ((0, 8), (1, 4))),
        "outgate_weight": gaussian(arg_keys[5], (D, VD), D ** -0.5, 0.125, ((0, 8), (1, 4))),
        "gate_down": gaussian(arg_keys[6], (D, RANK), D ** -0.5, 0.125),
        "gate_up": gaussian(arg_keys[7], (RANK, KD), RANK ** -0.5, 1.5, ((1, 4),), jnp.float32),
        "gate_bias": jnp.clip(0.5 + 4.0 * jax.random.uniform(arg_keys[8], (KD,), jnp.float32) ** shard_levels(arg_keys[8], (KD,), ((0, 4),), -0.2, 0.2), 0.5, 4.5),
        "group_gain": jnp.clip(1.0 + 0.1 * jax.random.normal(arg_keys[9], (VD,), jnp.float32), 0.5, 1.5),
        "proj_weight": gaussian(arg_keys[10], (VD, D), (VD // 4) ** -0.5, 0.25, ((0, 4), (1, 8))),
        "norm2_gain": jnp.clip(1.0 + 0.1 * jax.random.normal(arg_keys[11], (D,), jnp.float32), 0.5, 1.5),
        "ffn_gate": gaussian(arg_keys[12], (D, FF), D ** -0.5, 0.125, ((0, 8), (1, 4))),
        "ffn_up": gaussian(arg_keys[13], (D, FF), D ** -0.5, 0.125, ((0, 8), (1, 4))),
        "ffn_down": gaussian(arg_keys[14], (FF, D), (FF // 2) ** -0.5, 0.109375, ((0, 4), (1, 8))),
        "cotangent": gaussian(arg_keys[15], (TOKENS, D), 1.0, 6.0, ((0, 32),)),
    }


@jax.custom_vjp
def low(v):
    return lax.optimization_barrier(v.astype(jnp.bfloat16)).astype(jnp.float32)

@jax.custom_vjp
def low_back(v):
    return v

def low_keep(v):
    return (low(v), None)

def low_pass(kept, grad):
    return (grad,)

def back_keep(v):
    return (v, None)

def back_low(kept, grad):
    return (low(grad),)
low.defvjp(low_keep, low_pass)
low_back.defvjp(back_keep, back_low)
eps_norm = 1e-06
eps_group = 1.0
highest = lax.Precision.HIGHEST

def product(former, latter):
    return jnp.dot(former, latter, preferred_element_type=jnp.float32, precision=highest)

def block_step(carry_state, pieces):
    query_block, key_block, value_block, decay_block = pieces
    length = query_block.shape[0]
    running = jnp.cumsum(decay_block, axis=0)
    middle = running[length // 2]
    query_wide = query_block * jnp.exp(running - middle)
    key_wide = key_block * jnp.exp(middle - running)
    scores = product(query_wide, key_wide.T)
    causal = jnp.arange(length)[:, None] >= jnp.arange(length)[None, :]
    scores = jnp.where(causal, scores, 0.0)
    within = product(scores, value_block)
    across = product(query_block * jnp.exp(running), carry_state)
    final_sum = running[length - 1]
    carried = jnp.exp(final_sum)[:, None] * carry_state + product((key_block * jnp.exp(final_sum - running)).T, value_block)
    return (carried, within + across)

def mixer_sequence(pieces):
    query_seq, key_seq, value_seq, decay_seq = pieces
    blocks = query_seq.shape[0] // BLOCK
    key_width = query_seq.shape[1]
    value_width = value_seq.shape[1]
    initial = jnp.zeros((key_width, value_width), jnp.float32)
    stacked = (query_seq.reshape(blocks, BLOCK, key_width), key_seq.reshape(blocks, BLOCK, key_width), value_seq.reshape(blocks, BLOCK, value_width), decay_seq.reshape(blocks, BLOCK, key_width))
    _, result = lax.scan(jax.checkpoint(block_step), initial, stacked)
    return result.reshape(blocks * BLOCK, value_width)

def split_heads(array, width):
    count = array.shape[0] // LEN
    return array.reshape(count, LEN, HEADS, width).transpose(0, 2, 1, 3).reshape(count * HEADS, LEN, width)

def heads_mixer(queries, keys_rows, values_rows, log_decay):
    key_width = KD // HEADS
    value_width = VD // HEADS
    count = queries.shape[0] // LEN
    scaled = queries * key_width ** (-0.5)
    result = lax.map(mixer_sequence, (split_heads(scaled, key_width), split_heads(keys_rows, key_width), split_heads(values_rows, value_width), split_heads(log_decay, key_width)))
    return result.reshape(count, HEADS, LEN, value_width).transpose(0, 2, 1, 3).reshape(count * LEN, HEADS * value_width)

def rms_rows(rows, gain, eps):
    return rows * lax.rsqrt(lax.optimization_barrier(jnp.mean(rows * rows, axis=-1, keepdims=True)) + eps) * gain

def layer(inputs, norm1_gain, query_weight, key_weight, value_weight, outgate_weight, gate_down, gate_up, gate_bias, group_gain, proj_weight, norm2_gain, ffn_gate, ffn_up, ffn_down):
    normed_one = low(rms_rows(inputs, norm1_gain, eps_norm))
    queries = low_back(low(product(normed_one, query_weight)))
    keys_rows = low_back(low(product(normed_one, key_weight)))
    values_rows = low_back(low(product(normed_one, value_weight)))
    outgate = low_back(product(normed_one, outgate_weight))
    lowrank = low_back(product(normed_one, gate_down))
    log_decay = jax.nn.log_sigmoid(product(lowrank, gate_up) + gate_bias) / 16.0
    mixed = heads_mixer(queries, keys_rows, values_rows, log_decay)
    grouped = rms_rows(mixed.reshape(-1, HEADS, VD // HEADS), 1.0, eps_group)
    normed_heads = grouped.reshape(-1, VD) * group_gain
    gated = low(normed_heads * jax.nn.silu(outgate))
    resid = inputs + low_back(product(gated, proj_weight))
    normed_two = low(rms_rows(resid, norm2_gain, eps_norm))
    gate_pre = low_back(product(normed_two, ffn_gate))
    up_pre = low_back(product(normed_two, ffn_up))
    hidden = low(jax.nn.silu(gate_pre) * up_pre)
    return resid + product(hidden, ffn_down)

def reference(inputs, norm1_gain, query_weight, key_weight, value_weight, outgate_weight, gate_down, gate_up, gate_bias, group_gain, proj_weight, norm2_gain, ffn_gate, ffn_up, ffn_down, cotangent):
    floats = [array.astype(jnp.float32) for array in (inputs, norm1_gain, query_weight, key_weight, value_weight, outgate_weight, gate_down, gate_up, gate_bias, group_gain, proj_weight, norm2_gain, ffn_gate, ffn_up, ffn_down)]
    output, backward = jax.vjp(layer, *floats)
    grad_input, grad_norm1, grad_query, grad_key, grad_value, grad_outgate, grad_gate_down, grad_gate_up, grad_gate_bias, grad_group_gain, grad_proj, grad_norm2, grad_ffn_gate, grad_ffn_up, grad_ffn_down = backward(cotangent.astype(jnp.float32))
    return (output.astype(jnp.bfloat16), grad_input, grad_norm1, grad_query, grad_key, grad_value, grad_outgate, grad_gate_down, grad_gate_up, grad_gate_bias, grad_group_gain, grad_proj, grad_norm2, grad_ffn_gate, grad_ffn_up, grad_ffn_down)
```

```python
import functools

import jax
import jax.numpy as jnp
from jax import lax
from jax.experimental import pallas as pl
from jax.experimental.pallas import tpu as pltpu
from jax.sharding import PartitionSpec as P

BLOCK = 64
LEN = 1024
HIGHEST = lax.Precision.HIGHEST
EPS_NORM = 1e-06
EPS_GROUP = 1.0
BF = jnp.bfloat16
F32 = jnp.float32


def dot(a, b, ca, cb, precision=None):
    return lax.dot_general(
        a, b, (((ca,), (cb,)), ((), ())), precision=precision, preferred_element_type=F32
    )


def matmul(a, b):
    return dot(a, b, 1, 0)


def times_transposed(a, b):
    return dot(a, b, 1, 1)


def transposed_times(a, b):
    return dot(a, b, 0, 0)


def sigmoid(x):
    return 1.0 / (1.0 + jnp.exp(-x))


def causal(length, lower=True):
    rows = lax.broadcasted_iota(jnp.int32, (length, length), 0)
    columns = lax.broadcasted_iota(jnp.int32, (length, length), 1)
    return rows >= columns if lower else rows <= columns


def gates(lowrank, gate_up, gate_bias):
    logit = dot(lowrank, gate_up, 1, 0, HIGHEST) + gate_bias
    decay = (jnp.minimum(logit, 0.0) - jnp.log(1.0 + jnp.exp(-jnp.abs(logit)))) / 16.0
    ones = jnp.where(causal(BLOCK), 1.0, 0.0).astype(F32)
    return logit, dot(ones, decay, 1, 0, HIGHEST)


def forward_kernel(kw, vw, proj_ref, low_ref, up_ref, bias_ref, gain_ref,
                   gated_ref, mixed_ref, states_ref, state):
    blocks = proj_ref.shape[0] // BLOCK
    root = kw ** (-0.5)
    state[...] = jnp.zeros_like(state)
    mask = causal(BLOCK)

    def step(i, _):
        rows = pl.ds(pl.multiple_of(i * BLOCK, BLOCK), BLOCK)
        query = proj_ref[rows, 0:kw].astype(F32) * root
        key = proj_ref[rows, kw:2 * kw].astype(F32)
        value = proj_ref[rows, 2 * kw:2 * kw + vw]
        outgate = proj_ref[rows, 2 * kw + vw:2 * kw + 2 * vw].astype(F32)
        _, running = gates(low_ref[rows, :], up_ref[...], bias_ref[...])
        middle = running[BLOCK // 2:BLOCK // 2 + 1, :]
        last = running[BLOCK - 1:BLOCK, :]
        query_wide = (query * jnp.exp(running - middle)).astype(BF)
        key_wide = (key * jnp.exp(middle - running)).astype(BF)
        query_in = (query * jnp.exp(running)).astype(BF)
        key_out = (key * jnp.exp(last - running)).astype(BF)
        before = state[...]
        before_low = before.astype(BF)
        states_ref[i, :, :] = before_low
        scores = jnp.where(mask, times_transposed(query_wide, key_wide), 0.0).astype(BF)
        mixed = matmul(scores, value) + times_transposed(query_in, before_low)
        state[...] = before * jnp.exp(last) + transposed_times(value, key_out)
        mixed_ref[rows, :] = mixed.astype(mixed_ref.dtype)
        scale = lax.rsqrt(jnp.mean(mixed * mixed, axis=1, keepdims=True) + EPS_GROUP)
        normed = mixed * scale * gain_ref[...]
        gated_ref[rows, :] = (normed * (outgate * sigmoid(outgate))).astype(BF)
        return 0

    lax.fori_loop(0, blocks, step, 0)


def backward_kernel(kw, vw, proj_ref, low_ref, up_ref, bias_ref, gain_ref, mixed_ref,
                    states_ref, grad_ref, out_ref, down_ref, upgrad_ref, sums_ref, gains_ref, state):
    blocks = proj_ref.shape[0] // BLOCK
    root = kw ** (-0.5)
    state[...] = jnp.zeros_like(state)
    mask = causal(BLOCK)
    suffix = jnp.where(causal(BLOCK, False), 1.0, 0.0).astype(F32)
    upgrad_ref[...] = jnp.zeros_like(upgrad_ref)
    sums_ref[...] = jnp.zeros_like(sums_ref)
    gains_ref[...] = jnp.zeros_like(gains_ref)

    def step(j, _):
        i = blocks - 1 - j
        rows = pl.ds(pl.multiple_of(i * BLOCK, BLOCK), BLOCK)
        query = proj_ref[rows, 0:kw].astype(F32) * root
        key = proj_ref[rows, kw:2 * kw].astype(F32)
        value = proj_ref[rows, 2 * kw:2 * kw + vw]
        outgate = proj_ref[rows, 2 * kw + vw:2 * kw + 2 * vw].astype(F32)
        mixed = mixed_ref[rows, :].astype(F32)
        gain = gain_ref[...]
        grad_gated = grad_ref[rows, :].astype(F32)
        scale = lax.rsqrt(jnp.mean(mixed * mixed, axis=1, keepdims=True) + EPS_GROUP)
        unit = mixed * scale
        logistic = sigmoid(outgate)
        grad_normed = grad_gated * (outgate * logistic)
        out_ref[rows, 2 * kw + vw:2 * kw + 2 * vw] = (
            grad_gated * (unit * gain) * (logistic * (1.0 + outgate * (1.0 - logistic)))
        ).astype(BF)
        gains_ref[...] += jnp.sum(grad_normed * unit, axis=0, keepdims=True)
        weighted = grad_normed * gain
        grad = (scale * (weighted - unit * jnp.mean(weighted * unit, axis=1, keepdims=True))).astype(BF)
        low = low_ref[rows, :]
        logit, running = gates(low, up_ref[...], bias_ref[...])
        middle = running[BLOCK // 2:BLOCK // 2 + 1, :]
        last = running[BLOCK - 1:BLOCK, :]
        rise, fall = jnp.exp(running - middle), jnp.exp(middle - running)
        enter, leave = jnp.exp(running), jnp.exp(last - running)
        query_wide = (query * rise).astype(BF)
        key_wide = (key * fall).astype(BF)
        query_in = (query * enter).astype(BF)
        key_out = (key * leave).astype(BF)
        before = states_ref[i, :, :]
        after = state[...]
        after_low = after.astype(BF)
        carried = transposed_times(value, key_out)
        ended = before.astype(F32) * jnp.exp(last) + carried
        boundary = jnp.sum(ended * after, axis=0, keepdims=True)
        scores = jnp.where(mask, times_transposed(query_wide, key_wide), 0.0).astype(BF)
        grad_scores = jnp.where(mask, times_transposed(grad, value), 0.0).astype(BF)
        grad_value = transposed_times(scores, grad) + times_transposed(key_out, after_low)
        query_term = matmul(grad_scores, key_wide) * rise + matmul(grad, before) * enter
        key_term = transposed_times(grad_scores, query_wide) * fall + matmul(value, after_low) * leave
        state[...] = after * jnp.exp(last) + transposed_times(grad, query_in)
        out_ref[rows, 0:kw] = (query_term * root).astype(BF)
        out_ref[rows, kw:2 * kw] = key_term.astype(BF)
        out_ref[rows, 2 * kw:2 * kw + vw] = grad_value.astype(BF)
        grad_decay = dot(suffix, query * query_term - key * key_term, 1, 0, HIGHEST) + boundary
        grad_logit = grad_decay * (sigmoid(-logit) / 16.0)
        sums_ref[...] += jnp.sum(grad_logit, axis=0, keepdims=True)
        upgrad_ref[...] += dot(low, grad_logit, 0, 0, HIGHEST)
        down_ref[rows, :] = dot(grad_logit, up_ref[...], 1, 1, HIGHEST).astype(BF)
        return 0

    lax.fori_loop(0, blocks, step, 0)


def vmem():
    return pl.BlockSpec(memory_space=pltpu.VMEM)


def mixer_forward(proj, lowrank, gate_up, gate_bias, gain):
    rows, (rank, kw), vw = proj.shape[0], gate_up.shape, gain.shape[1]
    blocks = rows // BLOCK
    return pl.pallas_call(
        functools.partial(forward_kernel, kw, vw),
        out_shape=(
            jax.ShapeDtypeStruct((rows, vw), BF),
            jax.ShapeDtypeStruct((rows, vw), BF),
            jax.ShapeDtypeStruct((blocks, vw, kw), BF),
        ),
        in_specs=[vmem()] * 5,
        out_specs=(vmem(),) * 3,
        scratch_shapes=[pltpu.VMEM((vw, kw), F32)],
        compiler_params=pltpu.CompilerParams(vmem_limit_bytes=40 * 2**20),
        cost_estimate=pl.CostEstimate(flops=20_000_000_000, bytes_accessed=10 * 2**20, transcendentals=0),
        name="mixer_forward",
    )(proj, lowrank, gate_up, gate_bias, gain)


def mixer_backward(proj, lowrank, gate_up, gate_bias, gain, mixed, states, grad):
    rows, (rank, kw), vw = proj.shape[0], gate_up.shape, gain.shape[1]
    return pl.pallas_call(
        functools.partial(backward_kernel, kw, vw),
        out_shape=(
            jax.ShapeDtypeStruct(proj.shape, BF),
            jax.ShapeDtypeStruct((rows, rank), BF),
            jax.ShapeDtypeStruct((rank, kw), F32),
            jax.ShapeDtypeStruct((1, kw), F32),
            jax.ShapeDtypeStruct((1, vw), F32),
        ),
        in_specs=[vmem()] * 8,
        out_specs=(vmem(),) * 5,
        scratch_shapes=[pltpu.VMEM((vw, kw), F32)],
        compiler_params=pltpu.CompilerParams(vmem_limit_bytes=40 * 2**20),
        cost_estimate=pl.CostEstimate(flops=40_000_000_000, bytes_accessed=16 * 2**20, transcendentals=0),
        name="mixer_backward",
    )(proj, lowrank, gate_up, gate_bias, gain, mixed, states, grad)


def swap(array, axis, bit):
    size = lax.axis_size(axis)
    return lax.ppermute(array, axis, [(i, i ^ bit) for i in range(size)])


def reorder(array, dim):
    me, size = lax.axis_index("dp"), lax.axis_size("dp")
    width = array.shape[dim] // size
    return jnp.concatenate(
        [lax.dynamic_slice_in_dim(array, (j ^ me) * width, width, dim) for j in range(size)], dim
    )


def bits_of(size):
    return [1 << k for k in range(size.bit_length() - 1)]


def gather_bits(pieces, bits):
    for bit in bits:
        pieces.update({i ^ bit: swap(piece, "dp", bit) for i, piece in list(pieces.items())})
    return pieces


def scatter_bits(pieces, bits):
    for bit in bits:
        for i in [i for i in pieces if i & bit]:
            pieces[i ^ bit] = pieces[i ^ bit] + swap(pieces.pop(i), "dp", bit)
    return pieces


def in_order(pieces, dim):
    return jnp.concatenate([pieces[i] for i in range(len(pieces))], dim)


def cut(array, dim, count):
    return dict(enumerate(jnp.split(array, count, dim)))


def dp_orders():
    bits = bits_of(lax.axis_size("dp"))
    top, middle = bits[-1], bits[1:-1]
    return [[*middle, top, bits[0]], [top, *middle, bits[0]]]


def gather_dp(shard, dim):
    halves = [
        in_order(gather_bits({0: half}, order), dim)
        for half, order in zip(jnp.split(shard, 2, 1 - dim), dp_orders())
    ]
    return jnp.concatenate(halves, 1 - dim)


def scatter_dp(array, dim):
    halves = [
        scatter_bits(cut(half, dim, lax.axis_size("dp")), order[::-1])[0]
        for half, order in zip(jnp.split(array, 2, 1 - dim), dp_orders())
    ]
    return jnp.concatenate(halves, 1 - dim)


def crossed():
    high = lax.axis_index("tensor") // 2
    return high != lax.axis_index("dp") // (lax.axis_size("dp") // 2)


def gather_square(shard, dim):
    other = swap(shard, "tensor", 2)
    mine = jnp.where(crossed(), other, shard)
    give = jnp.where(crossed(), shard, other)
    bits = bits_of(lax.axis_size("dp"))
    pieces = {0: mine, bits[-1]: swap(give, "dp", bits[-1])}
    return in_order(gather_bits(pieces, [*bits[1:-1], bits[0]]), dim)


def scatter_square(array, dim):
    bits = bits_of(lax.axis_size("dp"))
    pieces = scatter_bits(cut(array, dim, lax.axis_size("dp")), [bits[0], *bits[1:-1][::-1]])
    mine, other = pieces[0], swap(pieces[bits[-1]], "dp", bits[-1])
    keep = jnp.where(crossed(), other, mine)
    send = jnp.where(crossed(), mine, other)
    return keep.astype(F32) + swap(send, "tensor", 2).astype(F32)


def across_y(array):
    return swap(array, "dp", lax.axis_size("dp") // 2)


def across_z(array):
    return swap(array, "tensor", 1)


def gather_tokens(own):
    half = own.shape[1] // 2
    left, right = own[:, :half], own[:, half:]
    y_right, z_right = across_y(left), across_z(right)
    z_left, d_right = across_z(left), across_z(y_right)
    y_left, d_left = across_y(right), across_y(z_right)
    return jnp.concatenate(
        [
            own,
            jnp.concatenate([z_left, z_right], 1),
            jnp.concatenate([y_left, y_right], 1),
            jnp.concatenate([d_left, d_right], 1),
        ],
        0,
    )


def scatter_tokens(partial):
    rows, half = partial.shape[0] // 4, partial.shape[1] // 2
    part = lambda r, c: partial[r * rows:(r + 1) * rows, c * half:(c + 1) * half]
    add = lambda a, b: a.astype(F32) + b.astype(F32)
    y_one, y_two = across_y(part(2, 0)), across_y(part(3, 0))
    z_one, z_two = across_z(part(1, 0)), across_z(part(3, 1))
    right = add(part(0, 1), y_one)
    left = add(part(0, 0), z_one)
    right = add(right, across_z(add(part(1, 1), y_two).astype(BF)))
    left = add(left, across_y(add(part(2, 1), z_two).astype(BF)))
    return jnp.concatenate([left, right], 1)


def everywhere(array, axes):
    for axis in axes:
        for bit in bits_of(lax.axis_size(axis)):
            array = array + swap(array, axis, bit)
    return array


def norm_scale(rows):
    return lax.rsqrt(jnp.mean(rows * rows, axis=1, keepdims=True) + EPS_NORM)


def norm_back(grad_normed, rows, scale, gain):
    weighted = grad_normed * gain
    return scale * weighted - rows * scale**3 * jnp.mean(weighted * rows, axis=1, keepdims=True)


def on_device(inputs, norm1_gain, query_weight, key_weight, value_weight, outgate_weight, gate_down,
              gate_up, gate_bias, group_gain, proj_weight, norm2_gain, ffn_gate, ffn_up, ffn_down, cotangent):
    head, heads = lax.axis_index("tensor"), lax.axis_size("tensor")
    own_rows = inputs.shape[0]
    units = ffn_gate.shape[1]
    kw, vw = query_weight.shape[1], value_weight.shape[1]
    inputs = reorder(inputs, 1)
    cotangent = reorder(cotangent, 1)
    gain_one = reorder(norm1_gain[None, :], 1)
    gain_two = reorder(norm2_gain[None, :], 1)
    gate_down = reorder(gate_down, 0)

    inputs_wide = inputs.astype(F32)
    scale_one = norm_scale(inputs_wide)
    normed_one = (inputs_wide * scale_one * gain_one).astype(BF)
    rows_one = lax.all_gather(normed_one, "tensor", axis=0, tiled=True)
    into = gather_dp(jnp.concatenate([query_weight, key_weight, value_weight, outgate_weight], 1), 0)
    shard_proj = jnp.concatenate([proj_weight] + [swap(proj_weight, "tensor", m) for m in range(1, heads)], 0)
    proj_full = gather_dp(shard_proj, 1)
    gate_up_full = gather_square(jnp.concatenate([ffn_gate, ffn_up], 1), 0)
    down_full = gather_square(ffn_down, 1)
    cot_rows = gather_tokens(cotangent)

    projected = matmul(rows_one, into).astype(BF)
    lowrank = matmul(rows_one, gate_down)
    gate_row, gain_row = gate_bias[None, :], group_gain[None, :]
    gated, mixed, states = mixer_forward(projected, lowrank, gate_up, gate_row, gain_row)
    def rows_of(array, index):
        return lax.dynamic_slice_in_dim(array, index * own_rows, own_rows, 0)
    gated_own = jnp.concatenate(
        [rows_of(gated, head)]
        + [swap(rows_of(gated, head ^ m), "tensor", m) for m in range(1, heads)],
        1,
    )
    resid = inputs_wide + matmul(gated_own, proj_full)
    scale_two = norm_scale(resid)
    normed_two = (resid * scale_two * gain_two).astype(BF)

    rows_two = gather_tokens(normed_two)
    pre = matmul(rows_two, gate_up_full)
    gate_pre, up_pre = pre[:, :units], pre[:, units:]
    logistic = sigmoid(gate_pre)
    act = gate_pre * logistic
    hidden = (act * up_pre).astype(BF)
    grad_hidden = times_transposed(cot_rows, down_full)
    grad_up = (grad_hidden * act).astype(BF)
    grad_gate = (grad_hidden * up_pre * (logistic * (1.0 + gate_pre * (1.0 - logistic)))).astype(BF)
    grad_pre = jnp.concatenate([grad_gate, grad_up], 1)
    grad_two = scatter_tokens(times_transposed(grad_pre, gate_up_full).astype(BF))
    norm2_term = jnp.sum(grad_two * resid * scale_two, axis=0, keepdims=True)
    grad_resid = cotangent.astype(F32) + norm_back(grad_two, resid, scale_two, gain_two)
    output = (resid + scatter_tokens(matmul(hidden, down_full).astype(BF))).astype(BF)
    grad_gate_up_own = scatter_square(transposed_times(rows_two, grad_pre).astype(BF), 0)
    grad_down_own = scatter_square(transposed_times(hidden, cot_rows).astype(BF), 1)

    grad_branch = grad_resid.astype(BF)
    grad_gated_own = times_transposed(grad_branch, proj_full).astype(BF)
    pieces = [grad_gated_own[:, m * vw:(m + 1) * vw] for m in range(heads)]
    pieces = jnp.stack([pieces[0]] + [swap(pieces[m], "tensor", m) for m in range(1, heads)], 0)
    grad_gated = jnp.concatenate(
        [lax.dynamic_index_in_dim(pieces, head ^ t, 0, keepdims=False) for t in range(heads)], 0
    )
    grad_into, grad_low, up_term, bias_term, group_term = mixer_backward(
        projected, lowrank, gate_up, gate_row, gain_row, mixed, states, grad_gated
    )
    grad_proj_part = cut(scatter_dp(transposed_times(gated_own, grad_branch).astype(BF), 1), 0, heads)
    grad_proj = grad_proj_part[0].astype(F32)
    for m in range(1, heads):
        grad_proj = grad_proj + swap(grad_proj_part[m], "tensor", m).astype(F32)
    grad_into_own = scatter_dp(transposed_times(rows_one, grad_into).astype(BF), 0).astype(F32)
    total = (times_transposed(grad_into, into) + times_transposed(grad_low, gate_down)).astype(BF)
    norm1_term = jnp.sum(total.astype(F32) * rows_one.astype(F32), axis=0, keepdims=True) / gain_one
    down_term = transposed_times(grad_low, rows_one)
    grad_one = lax.psum_scatter(total, "tensor", scatter_dimension=0, tiled=True).astype(F32)
    grad_input = grad_resid + norm_back(grad_one, inputs_wide, scale_one, gain_one)

    summed = everywhere(reorder(jnp.concatenate([down_term, norm1_term, norm2_term], 0), 1), ("dp", "tensor"))
    rank = gate_down.shape[1]
    by_head = everywhere(
        jnp.concatenate([up_term, bias_term, group_term[:, :kw], group_term[:, kw:]], 0), ("dp",)
    )
    splits = [kw, 2 * kw, 2 * kw + vw]
    grad_query, grad_key, grad_value, grad_outgate = jnp.split(grad_into_own, splits, 1)
    return (
        reorder(output, 1),
        reorder(grad_input, 1),
        summed[rank],
        grad_query,
        grad_key,
        grad_value,
        grad_outgate,
        summed[:rank].T,
        by_head[:rank],
        by_head[rank],
        by_head[rank + 1:].reshape(-1),
        grad_proj,
        summed[rank + 1],
        grad_gate_up_own[:, :units],
        grad_gate_up_own[:, units:],
        grad_down_own,
    )


def solution(mesh):
    tokens, whole = P(("dp", "tensor"), None), P()
    rows, columns = P("dp", "tensor"), P("tensor", "dp")
    last = P(None, "tensor")
    head = P("tensor")
    return jax.shard_map(
        on_device,
        mesh=mesh,
        in_specs=(tokens, whole, rows, rows, rows, rows, whole, last, head, head, columns, whole, rows, rows,
                  columns, tokens),
        out_specs=(tokens, tokens, whole, rows, rows, rows, rows, whole, last, head, head, columns, whole, rows,
                   rows, columns),
        check_vma=False,
    )
```

```python
import functools

import jax
import jax.numpy as jnp
from jax import lax
from jax.experimental import pallas as pl
from jax.experimental.pallas import tpu as pltpu
from jax.sharding import PartitionSpec as P

BLOCK = 64
LEN = 1024
LANES = 128
HIGHEST = lax.Precision.HIGHEST
EPS_NORM = 1e-06
EPS_GROUP = 1.0
BF = jnp.bfloat16
F32 = jnp.float32


def dot(a, b, ca, cb, precision=None):
    return lax.dot_general(
        a, b, (((ca,), (cb,)), ((), ())), precision=precision, preferred_element_type=F32
    )


def matmul(a, b):
    return dot(a, b, 1, 0)


def times_transposed(a, b):
    return dot(a, b, 1, 1)


def transposed_times(a, b):
    return dot(a, b, 0, 0)


def sigmoid(x):
    return 1.0 / (1.0 + jnp.exp(-x))


def causal(length, lower=True):
    rows = lax.broadcasted_iota(jnp.int32, (length, length), 0)
    columns = lax.broadcasted_iota(jnp.int32, (length, length), 1)
    return rows >= columns if lower else rows <= columns


def gates(lowrank, gate_up, gate_bias):
    logit = dot(lowrank, gate_up, 1, 0, HIGHEST) + gate_bias
    decay = (jnp.minimum(logit, 0.0) - jnp.log(1.0 + jnp.exp(-jnp.abs(logit)))) / 16.0
    ones = jnp.where(causal(BLOCK), 1.0, 0.0).astype(F32)
    return logit, dot(ones, decay, 1, 0, HIGHEST)


def forward_kernel(kw, vw, proj_ref, low_ref, up_ref, bias_ref, gain_ref,
                   gated_ref, mixed_ref, states_ref, state):
    blocks = proj_ref.shape[0] // BLOCK
    root = kw ** (-0.5)
    state[...] = jnp.zeros_like(state)
    mask = causal(BLOCK)

    def step(i, _):
        rows = pl.ds(pl.multiple_of(i * BLOCK, BLOCK), BLOCK)
        query = proj_ref[rows, 0:kw].astype(F32) * root
        key = proj_ref[rows, kw:2 * kw].astype(F32)
        value = proj_ref[rows, 2 * kw:2 * kw + vw]
        outgate = proj_ref[rows, 2 * kw + vw:2 * kw + 2 * vw].astype(F32)
        _, running = gates(low_ref[rows, :], up_ref[...], bias_ref[...])
        middle = running[BLOCK // 2:BLOCK // 2 + 1, :]
        last = running[BLOCK - 1:BLOCK, :]
        query_wide = (query * jnp.exp(running - middle)).astype(BF)
        key_wide = (key * jnp.exp(middle - running)).astype(BF)
        query_in = (query * jnp.exp(running)).astype(BF)
        key_out = (key * jnp.exp(last - running)).astype(BF)
        before = state[...]
        before_low = before.astype(BF)
        states_ref[i, :, :] = before_low
        scores = jnp.where(mask, times_transposed(query_wide, key_wide), 0.0).astype(BF)
        mixed = matmul(scores, value) + times_transposed(query_in, before_low)
        state[...] = before * jnp.exp(last) + transposed_times(value, key_out)
        mixed_ref[rows, :] = mixed.astype(mixed_ref.dtype)
        scale = lax.rsqrt(jnp.mean(mixed * mixed, axis=1, keepdims=True) + EPS_GROUP)
        normed = mixed * scale * gain_ref[...]
        gated_ref[rows, :] = (normed * (outgate * sigmoid(outgate))).astype(BF)
        return 0

    lax.fori_loop(0, blocks, step, 0)


def backward_kernel(kw, vw, proj_ref, low_ref, up_ref, bias_ref, gain_ref, mixed_ref,
                    states_ref, grad_ref, wide_ref, out_ref, upgrad_ref, sums_ref, gains_ref, state):
    blocks = proj_ref.shape[0] // BLOCK
    root = kw ** (-0.5)
    state[...] = jnp.zeros_like(state)
    mask = causal(BLOCK)
    suffix = jnp.where(causal(BLOCK, False), 1.0, 0.0).astype(F32)
    upgrad_ref[...] = jnp.zeros_like(upgrad_ref)
    sums_ref[...] = jnp.zeros_like(sums_ref)
    gains_ref[...] = jnp.zeros_like(gains_ref)

    def step(j, _):
        i = blocks - 1 - j
        rows = pl.ds(pl.multiple_of(i * BLOCK, BLOCK), BLOCK)
        query = proj_ref[rows, 0:kw].astype(F32) * root
        key = proj_ref[rows, kw:2 * kw].astype(F32)
        value = proj_ref[rows, 2 * kw:2 * kw + vw]
        outgate = proj_ref[rows, 2 * kw + vw:2 * kw + 2 * vw].astype(F32)
        mixed = mixed_ref[rows, :].astype(F32)
        gain = gain_ref[...]
        grad_gated = grad_ref[rows, :].astype(F32)
        scale = lax.rsqrt(jnp.mean(mixed * mixed, axis=1, keepdims=True) + EPS_GROUP)
        unit = mixed * scale
        logistic = sigmoid(outgate)
        grad_normed = grad_gated * (outgate * logistic)
        out_ref[rows, 2 * kw + vw:2 * kw + 2 * vw] = (
            grad_gated * (unit * gain) * (logistic * (1.0 + outgate * (1.0 - logistic)))
        ).astype(BF)
        gains_ref[...] += jnp.sum(grad_normed * unit, axis=0, keepdims=True)
        weighted = grad_normed * gain
        grad = (scale * (weighted - unit * jnp.mean(weighted * unit, axis=1, keepdims=True))).astype(BF)
        low = low_ref[rows, :]
        logit, running = gates(low, up_ref[...], bias_ref[...])
        middle = running[BLOCK // 2:BLOCK // 2 + 1, :]
        last = running[BLOCK - 1:BLOCK, :]
        rise, fall = jnp.exp(running - middle), jnp.exp(middle - running)
        enter, leave = jnp.exp(running), jnp.exp(last - running)
        query_wide = (query * rise).astype(BF)
        key_wide = (key * fall).astype(BF)
        query_in = (query * enter).astype(BF)
        key_out = (key * leave).astype(BF)
        before = states_ref[i, :, :]
        after = state[...]
        after_low = after.astype(BF)
        carried = transposed_times(value, key_out)
        ended = before.astype(F32) * jnp.exp(last) + carried
        boundary = jnp.sum(ended * after, axis=0, keepdims=True)
        scores = jnp.where(mask, times_transposed(query_wide, key_wide), 0.0).astype(BF)
        grad_scores = jnp.where(mask, times_transposed(grad, value), 0.0).astype(BF)
        grad_value = transposed_times(scores, grad) + times_transposed(key_out, after_low)
        query_term = matmul(grad_scores, key_wide) * rise + matmul(grad, before) * enter
        key_term = transposed_times(grad_scores, query_wide) * fall + matmul(value, after_low) * leave
        state[...] = after * jnp.exp(last) + transposed_times(grad, query_in)
        out_ref[rows, 0:kw] = (query_term * root).astype(BF)
        out_ref[rows, kw:2 * kw] = key_term.astype(BF)
        out_ref[rows, 2 * kw:2 * kw + vw] = grad_value.astype(BF)
        grad_decay = dot(suffix, query * query_term - key * key_term, 1, 0, HIGHEST) + boundary
        grad_logit = grad_decay * (sigmoid(-logit) / 16.0)
        sums_ref[...] += jnp.sum(grad_logit, axis=0, keepdims=True)
        upgrad_ref[...] += dot(low, grad_logit, 0, 0, HIGHEST)
        out_ref[rows, 2 * kw + 2 * vw:] = dot(grad_logit, wide_ref[...], 1, 1, HIGHEST).astype(BF)
        return 0

    lax.fori_loop(0, blocks, step, 0)


def vmem():
    return pl.BlockSpec(memory_space=pltpu.VMEM)


def mixer_forward(proj, lowrank, gate_up, gate_bias, gain):
    rows, (rank, kw), vw = proj.shape[0], gate_up.shape, gain.shape[1]
    blocks = rows // BLOCK
    return pl.pallas_call(
        functools.partial(forward_kernel, kw, vw),
        out_shape=(
            jax.ShapeDtypeStruct((rows, vw), BF),
            jax.ShapeDtypeStruct((rows, vw), BF),
            jax.ShapeDtypeStruct((blocks, vw, kw), BF),
        ),
        in_specs=[vmem()] * 5,
        out_specs=(vmem(),) * 3,
        scratch_shapes=[pltpu.VMEM((vw, kw), F32)],
        compiler_params=pltpu.CompilerParams(vmem_limit_bytes=40 * 2**20),
        cost_estimate=pl.CostEstimate(flops=20_000_000_000, bytes_accessed=10 * 2**20, transcendentals=0),
        name="mixer_forward",
    )(proj, lowrank, gate_up, gate_bias, gain)


def mixer_backward(proj, lowrank, gate_up, gate_bias, gain, mixed, states, grad):
    rows, (rank, kw), vw = proj.shape[0], gate_up.shape, gain.shape[1]
    wide = jnp.pad(gate_up, ((0, LANES - rank), (0, 0)))
    return pl.pallas_call(
        functools.partial(backward_kernel, kw, vw),
        out_shape=(
            jax.ShapeDtypeStruct((rows, proj.shape[1] + LANES), BF),
            jax.ShapeDtypeStruct((rank, kw), F32),
            jax.ShapeDtypeStruct((1, kw), F32),
            jax.ShapeDtypeStruct((1, vw), F32),
        ),
        in_specs=[vmem()] * 9,
        out_specs=(vmem(),) * 4,
        scratch_shapes=[pltpu.VMEM((vw, kw), F32)],
        compiler_params=pltpu.CompilerParams(vmem_limit_bytes=40 * 2**20),
        cost_estimate=pl.CostEstimate(flops=40_000_000_000, bytes_accessed=16 * 2**20, transcendentals=0),
        name="mixer_backward",
    )(proj, lowrank, gate_up, gate_bias, gain, mixed, states, grad, wide)


def swap(array, axis, bit):
    size = lax.axis_size(axis)
    return lax.ppermute(array, axis, [(i, i ^ bit) for i in range(size)])


def bits_of(size):
    return [1 << k for k in range(size.bit_length() - 1)]


def dp_bits():
    bits = bits_of(lax.axis_size("dp"))
    return bits[:1], bits[1:-1], bits[-1:]


def index_at(place):
    low, middle, top = dp_bits()
    return sum(bit for k, bit in enumerate([*middle, *top, *low]) if place >> k & 1)


def reorder(array, dim, back=False):
    me, size = lax.axis_index("dp"), lax.axis_size("dp")
    width = array.shape[dim] // size
    to = [0] * size
    for place in range(size):
        to[index_at(place)] = place
    places = []
    for p in range(size):
        if back:
            source = jnp.asarray(to, jnp.int32)[p ^ me]
        else:
            source = index_at(p) ^ me
        places.append(lax.dynamic_slice_in_dim(array, source * width, width, dim))
    return jnp.concatenate(places, dim)


class Flow:
    def __init__(self):
        self.fence, self.posted = (), []

    def send(self, array, axis, bit):
        got = swap(lax.optimization_barrier((array, self.fence))[0] if self.fence else array, axis, bit)
        self.posted.append(got)
        return got

    def note(self, *arrays):
        self.posted += arrays

    def turn(self):
        self.fence, self.posted = tuple(self.posted), []

    def held(self, array):
        return lax.optimization_barrier((array, self.fence))[0]


def after(array, *earlier):
    return lax.optimization_barrier((array, earlier))[0]


def pick(array, dim, count, places):
    width = array.shape[dim] // count
    return jnp.concatenate([lax.slice_in_dim(array, p * width, (p + 1) * width, axis=dim) for p in places], dim)


def grow(flow, array, bits, dim):
    for bit in bits:
        array = jnp.concatenate([array, flow.send(array, "dp", bit)], dim)
    return array


def turned(array, dim):
    count = lax.axis_size("dp") // 2
    return pick(array, dim, count, [*range(0, count, 2), *range(1, count, 2)])


def turned_back(array, dim):
    count = lax.axis_size("dp") // 2
    return pick(array, dim, count, [p for k in range(count // 2) for p in (k, count // 2 + k)])


def shrink(flow, array, bits, dim):
    for bit in bits:
        keep, give = jnp.split(array, 2, dim)
        array = keep + flow.send(give, "dp", bit)
    return array


def shrink_inner(flow, array, bits, dim):
    for bit in reversed(bits):
        keep = pick(array, dim, 4, [0, 2])
        give = pick(array, dim, 4, [1, 3])
        array = keep + flow.send(give, "dp", bit)
    return array


def gather_first(flow, one, two, dim):
    low, middle, top = dp_bits()
    return grow(flow, one, middle, dim), grow(flow, two, top, dim)


def gather_second(flow, one, two, dim):
    low, middle, top = dp_bits()
    return grow(flow, one, top, dim), turned(grow(flow, two, middle, dim), dim)


def gather_core(flow, one, two, dim):
    low, middle, top = dp_bits()
    return grow(flow, one, low, dim), grow(flow, two, low, dim)


def scatter_core(flow, one, two, dim):
    low, middle, top = dp_bits()
    return shrink(flow, one, low, dim), shrink(flow, two, low, dim)


def scatter_first(flow, one, two, dim):
    low, middle, top = dp_bits()
    return shrink(flow, one, top, dim), shrink_inner(flow, two, middle, dim)


def scatter_second(flow, one, two, dim):
    low, middle, top = dp_bits()
    return shrink(flow, one, middle[::-1], dim), shrink(flow, two, top, dim)


def gather_rows(array):
    return lax.all_gather(array, "tensor", axis=0, tiled=True)


def scatter_rows(array):
    return lax.psum_scatter(array, "tensor", scatter_dimension=0, tiled=True)


class Everywhere:
    def __init__(self, flow, array, axes):
        self.flow, self.array = flow, array
        self.left = [(axis, bit) for axis in axes for bit in bits_of(lax.axis_size(axis))]

    def step(self, count=1):
        for axis, bit in self.left[:count]:
            self.array = self.array + self.flow.send(self.array, axis, bit)
        self.left = self.left[count:]


def norm_scale(rows):
    return lax.rsqrt(jnp.mean(rows * rows, axis=1, keepdims=True) + EPS_NORM)


def norm_back(grad_normed, rows, scale, gain):
    weighted = grad_normed * gain
    return scale * weighted - rows * scale**3 * jnp.mean(weighted * rows, axis=1, keepdims=True)


def on_device(inputs, norm1_gain, query_weight, key_weight, value_weight, outgate_weight, gate_down,
              gate_up, gate_bias, group_gain, proj_weight, norm2_gain, ffn_gate, ffn_up, ffn_down, cotangent):
    head, heads = lax.axis_index("tensor"), lax.axis_size("tensor")
    own_rows = inputs.shape[0]
    units = ffn_gate.shape[1]
    kw, vw = query_weight.shape[1], value_weight.shape[1]
    inputs = reorder(inputs, 1)
    cotangent = reorder(cotangent, 1)
    gain_one = reorder(norm1_gain[None, :], 1)
    gain_two = reorder(norm2_gain[None, :], 1)
    gate_down = reorder(gate_down, 0)

    flow = Flow()
    inputs_wide = inputs.astype(F32)
    scale_one = norm_scale(inputs_wide)
    normed_one = (inputs_wide * scale_one * gain_one).astype(BF)

    shard_proj = gather_rows(proj_weight)
    rows_one = gather_rows(normed_one)
    into_shard = jnp.concatenate([query_weight, key_weight, value_weight, outgate_weight], 1)
    into = gather_first(flow, *jnp.split(into_shard, 2, 1), 0)
    flow.turn()
    into = gather_second(flow, *into, 0)
    flow.turn()
    into = gather_core(flow, *into, 0)
    flow.turn()
    proj_full = gather_first(flow, *jnp.split(shard_proj, 2, 0), 1)
    flow.turn()
    proj_full = gather_second(flow, *proj_full, 1)
    flow.turn()
    gate_up_full = gather_first(flow, ffn_gate, ffn_up, 0)
    proj_full = jnp.concatenate(gather_core(flow, *proj_full, 1), 0)
    flow.turn()
    cot_rows = gather_rows(after(cotangent, shard_proj)).reshape(heads, 2, own_rows // 2, -1)
    cot_rows = [cot_rows[:, k].reshape(heads * own_rows // 2, -1) for k in range(2)]

    down_wide = jnp.pad(gate_down, ((0, 0), (0, LANES - gate_down.shape[1])))
    into = jnp.concatenate([*into, down_wide], 1)
    projected = matmul(flow.held(rows_one), into[:, :2 * kw + 2 * vw]).astype(BF)
    lowrank = matmul(rows_one, gate_down)
    gate_row, gain_row = gate_bias[None, :], group_gain[None, :]
    gated, mixed, states = mixer_forward(projected, lowrank, gate_up, gate_row, gain_row)
    flow.note(gated)
    flow.turn()

    def exchange(pieces, dim):
        come = jnp.stack([pieces[0]] + [swap(pieces[m], "tensor", m) for m in range(1, heads)], 0)
        return jnp.concatenate(
            [lax.dynamic_index_in_dim(come, head ^ t, 0, keepdims=False) for t in range(heads)], dim
        )
    def rows_of(array, index):
        return lax.dynamic_slice_in_dim(array, index * own_rows, own_rows, 0)
    gated_own = exchange([rows_of(gated, head ^ m) for m in range(heads)], 1)
    gate_up_full = gather_second(flow, *gate_up_full, 0)
    flow.turn()
    resid = inputs_wide + lax.optimization_barrier(matmul(flow.held(after(gated_own, cot_rows)), proj_full))
    scale_two = norm_scale(resid)
    normed_two = (resid * scale_two * gain_two).astype(BF)
    rows_two = [gather_rows(part) for part in jnp.split(normed_two, 2, 0)]
    flow.note(normed_two)
    flow.turn()

    gate_full, up_full = gather_core(flow, *gate_up_full, 0)
    down_full = gather_first(flow, *jnp.split(ffn_down, 2, 0), 1)
    flow.turn()
    down_full = gather_second(flow, *down_full, 1)
    flow.turn()
    down_full = jnp.concatenate(gather_core(flow, *down_full, 1), 0)
    flow.turn()

    def feed_forward(rows, cot):
        gate_pre = matmul(rows, gate_full)
        up_pre = matmul(rows, up_full)
        logistic = sigmoid(gate_pre)
        act = gate_pre * logistic
        hidden = (act * up_pre).astype(BF)
        grad_hidden = times_transposed(cot, down_full)
        grad_up = (grad_hidden * act).astype(BF)
        grad_gate = (grad_hidden * up_pre * (logistic * (1.0 + gate_pre * (1.0 - logistic)))).astype(BF)
        back = (times_transposed(grad_gate, gate_full) + times_transposed(grad_up, up_full)).astype(BF)
        return hidden, grad_gate, grad_up, back
    first = feed_forward(rows_two[0], cot_rows[0])
    rows_two[1] = after(rows_two[1], first[3])
    hidden, grad_gate, grad_up, part_two = zip(first, feed_forward(rows_two[1], cot_rows[1]))

    grad_two = jnp.concatenate([scatter_rows(part) for part in part_two], 0).astype(F32)
    hidden, grad_gate, grad_up, rows_two, cot_rows = (
        jnp.concatenate(parts, 0) for parts in (hidden, grad_gate, grad_up, rows_two, cot_rows)
    )
    flow.note(part_two)
    flow.turn()
    gate_sums = transposed_times(rows_two, flow.held(grad_gate)).astype(BF)
    up_sums = transposed_times(rows_two, flow.held(grad_up)).astype(BF)
    gate_sums, up_sums = scatter_core(flow, gate_sums, up_sums, 0)
    flow.turn()
    gate_sums, up_sums = scatter_first(flow, gate_sums, up_sums, 0)
    down_sums = transposed_times(after(hidden, part_two), cot_rows).astype(BF)
    part_out = matmul(after(hidden, part_two), down_full).astype(BF)
    out_own = [scatter_rows(part) for part in jnp.split(part_out, 2, 0)]
    flow.note(part_out, down_sums)
    flow.turn()
    grad_two = flow.held(grad_two)
    norm2_term = jnp.sum(grad_two * resid * scale_two, axis=0, keepdims=True)
    grad_resid = cotangent.astype(F32) + norm_back(grad_two, resid, scale_two, gain_two)

    grad_branch = grad_resid.astype(BF)
    grad_gated_own = times_transposed(grad_branch, proj_full).astype(BF)
    flow.note(grad_gated_own)
    flow.turn()
    grad_gated = exchange(
        [lax.dynamic_slice_in_dim(grad_gated_own, (head ^ m) * vw, vw, 1) for m in range(heads)], 0
    )
    gate_sums, up_sums = scatter_second(flow, gate_sums, up_sums, 0)
    grad_gate_own, grad_up_own = gate_sums.astype(F32), up_sums.astype(F32)
    proj_sums = transposed_times(gated_own, flow.held(grad_branch)).astype(BF)
    proj_sums = scatter_core(flow, *jnp.split(proj_sums, 2, 0), 1)
    flow.turn()
    proj_sums = scatter_first(flow, *proj_sums, 1)

    grad_into, up_term, bias_term, group_term = mixer_backward(
        projected, lowrank, gate_up, gate_row, gain_row, mixed, states, flow.held(grad_gated)
    )
    grad_low = grad_into[:, 2 * kw + 2 * vw:2 * kw + 2 * vw + gate_down.shape[1]]
    flow.note(grad_into)
    flow.turn()
    output = (resid + jnp.concatenate(flow.held(out_own), 0).astype(F32)).astype(BF)
    total_low = times_transposed(grad_into, into).astype(BF)
    grad_one = scatter_rows(total_low).astype(F32)
    proj_sums = scatter_second(flow, *proj_sums, 1)
    flow.note(total_low)
    flow.turn()
    into_sums = transposed_times(rows_one, flow.held(grad_into)).astype(BF)
    into_sums = scatter_core(flow, *jnp.split(into_sums[:, :2 * kw + 2 * vw], 2, 1), 0)
    flow.turn()
    into_sums = scatter_first(flow, *into_sums, 0)
    norm1_term = jnp.sum(flow.held(total_low).astype(F32) * rows_one.astype(F32), axis=0, keepdims=True) / gain_one
    down_term = transposed_times(grad_low, rows_one)
    small = Everywhere(
        flow, reorder(jnp.concatenate([down_term, norm1_term, norm2_term], 0), 1, True), ("dp", "tensor")
    )
    by_head = Everywhere(
        flow, jnp.concatenate([up_term, bias_term, group_term[:, :kw], group_term[:, kw:]], 0), ("dp",)
    )
    by_head.step()
    flow.note(small.array)
    flow.turn()
    into_sums = scatter_second(flow, *into_sums, 0)
    small.step()
    by_head.step()
    flow.turn()
    down_sums = scatter_core(flow, *jnp.split(down_sums, 2, 0), 1)
    small.step()
    by_head.step(len(by_head.left))
    flow.turn()
    down_sums = scatter_first(flow, *down_sums, 1)
    small.step()
    flow.note(grad_one)
    flow.turn()
    down_sums = scatter_second(flow, *down_sums, 1)
    small.step(len(small.left) - 1)
    flow.turn()
    small.step(len(small.left))
    proj_sums = jnp.concatenate(proj_sums, 0)
    grad_proj = lax.dynamic_slice_in_dim(proj_sums, head * vw, vw, 0).astype(F32)
    for m in range(1, heads):
        part = lax.dynamic_slice_in_dim(proj_sums, (head ^ m) * vw, vw, 0)
        grad_proj = grad_proj + flow.send(part, "tensor", m).astype(F32)
    grad_into_own = jnp.concatenate(into_sums, 1).astype(F32)
    grad_down_own = jnp.concatenate(down_sums, 0).astype(F32)
    grad_input = grad_resid + norm_back(grad_one, inputs_wide, scale_one, gain_one)
    summed, by_head = small.array, by_head.array
    rank = gate_down.shape[1]
    splits = [kw, 2 * kw, 2 * kw + vw]
    grad_query, grad_key, grad_value, grad_outgate = jnp.split(grad_into_own, splits, 1)
    return (
        reorder(output, 1, True),
        reorder(grad_input, 1, True),
        summed[rank],
        grad_query,
        grad_key,
        grad_value,
        grad_outgate,
        summed[:rank].T,
        by_head[:rank],
        by_head[rank],
        by_head[rank + 1:].reshape(-1),
        grad_proj,
        summed[rank + 1],
        grad_gate_own,
        grad_up_own,
        grad_down_own,
    )


def solution(mesh):
    tokens, whole = P(("dp", "tensor"), None), P()
    rows, columns = P("dp", "tensor"), P("tensor", "dp")
    last = P(None, "tensor")
    head = P("tensor")
    return jax.shard_map(
        on_device,
        mesh=mesh,
        in_specs=(tokens, whole, rows, rows, rows, rows, whole, last, head, head, columns, whole, rows, rows,
                  columns, tokens),
        out_specs=(tokens, tokens, whole, rows, rows, rows, rows, whole, last, head, head, columns, whole, rows,
                   rows, columns),
        check_vma=False,
    )
```

```python
import functools

import jax
import jax.numpy as jnp
from jax import lax
from jax.experimental import pallas as pl
from jax.experimental.pallas import tpu as pltpu
from jax.sharding import PartitionSpec as P

BLOCK = 64
LEN = 1024
LANES = 128
HIGHEST = lax.Precision.HIGHEST
EPS_NORM = 1e-06
EPS_GROUP = 1.0
BF = jnp.bfloat16
F32 = jnp.float32


def dot(a, b, ca, cb, precision=None):
    return lax.dot_general(
        a, b, (((ca,), (cb,)), ((), ())), precision=precision, preferred_element_type=F32
    )


def matmul(a, b):
    return dot(a, b, 1, 0)


def times_transposed(a, b):
    return dot(a, b, 1, 1)


def transposed_times(a, b):
    return dot(a, b, 0, 0)


def sigmoid(x):
    return 1.0 / (1.0 + jnp.exp(-x))


def causal(length, lower=True):
    rows = lax.broadcasted_iota(jnp.int32, (length, length), 0)
    columns = lax.broadcasted_iota(jnp.int32, (length, length), 1)
    return rows >= columns if lower else rows <= columns


def gates(lowrank, gate_up, gate_bias):
    logit = dot(lowrank, gate_up, 1, 0, HIGHEST) + gate_bias
    decay = (jnp.minimum(logit, 0.0) - jnp.log(1.0 + jnp.exp(-jnp.abs(logit)))) / 16.0
    ones = jnp.where(causal(BLOCK), 1.0, 0.0).astype(F32)
    return logit, dot(ones, decay, 1, 0, HIGHEST)


def forward_kernel(kw, vw, proj_ref, low_ref, up_ref, bias_ref, gain_ref,
                   gated_ref, mixed_ref, states_ref, state):
    blocks = proj_ref.shape[0] // BLOCK
    root = kw ** (-0.5)
    state[...] = jnp.zeros_like(state)
    mask = causal(BLOCK)

    def step(i, _):
        rows = pl.ds(pl.multiple_of(i * BLOCK, BLOCK), BLOCK)
        query = proj_ref[rows, 0:kw].astype(F32) * root
        key = proj_ref[rows, kw:2 * kw].astype(F32)
        value = proj_ref[rows, 2 * kw:2 * kw + vw]
        outgate = proj_ref[rows, 2 * kw + vw:2 * kw + 2 * vw].astype(F32)
        _, running = gates(low_ref[rows, :], up_ref[...], bias_ref[...])
        middle = running[BLOCK // 2:BLOCK // 2 + 1, :]
        last = running[BLOCK - 1:BLOCK, :]
        query_wide = (query * jnp.exp(running - middle)).astype(BF)
        key_wide = (key * jnp.exp(middle - running)).astype(BF)
        query_in = (query * jnp.exp(running)).astype(BF)
        key_out = (key * jnp.exp(last - running)).astype(BF)
        before = state[...]
        before_low = before.astype(BF)
        states_ref[i, :, :] = before_low
        scores = jnp.where(mask, times_transposed(query_wide, key_wide), 0.0).astype(BF)
        mixed = matmul(scores, value) + times_transposed(query_in, before_low)
        state[...] = before * jnp.exp(last) + transposed_times(value, key_out)
        mixed_ref[rows, :] = mixed.astype(mixed_ref.dtype)
        scale = lax.rsqrt(jnp.mean(mixed * mixed, axis=1, keepdims=True) + EPS_GROUP)
        normed = mixed * scale * gain_ref[...]
        gated_ref[rows, :] = (normed * (outgate * sigmoid(outgate))).astype(BF)
        return 0

    lax.fori_loop(0, blocks, step, 0)


def backward_kernel(kw, vw, proj_ref, low_ref, up_ref, bias_ref, gain_ref, mixed_ref,
                    states_ref, grad_ref, wide_ref, out_ref, upgrad_ref, sums_ref, gains_ref, state):
    blocks = proj_ref.shape[0] // BLOCK
    root = kw ** (-0.5)
    state[...] = jnp.zeros_like(state)
    mask = causal(BLOCK)
    suffix = jnp.where(causal(BLOCK, False), 1.0, 0.0).astype(F32)
    upgrad_ref[...] = jnp.zeros_like(upgrad_ref)
    sums_ref[...] = jnp.zeros_like(sums_ref)
    gains_ref[...] = jnp.zeros_like(gains_ref)

    def step(j, _):
        i = blocks - 1 - j
        rows = pl.ds(pl.multiple_of(i * BLOCK, BLOCK), BLOCK)
        query = proj_ref[rows, 0:kw].astype(F32) * root
        key = proj_ref[rows, kw:2 * kw].astype(F32)
        value = proj_ref[rows, 2 * kw:2 * kw + vw]
        outgate = proj_ref[rows, 2 * kw + vw:2 * kw + 2 * vw].astype(F32)
        mixed = mixed_ref[rows, :].astype(F32)
        gain = gain_ref[...]
        grad_gated = grad_ref[rows, :].astype(F32)
        scale = lax.rsqrt(jnp.mean(mixed * mixed, axis=1, keepdims=True) + EPS_GROUP)
        unit = mixed * scale
        logistic = sigmoid(outgate)
        grad_normed = grad_gated * (outgate * logistic)
        out_ref[rows, 2 * kw + vw:2 * kw + 2 * vw] = (
            grad_gated * (unit * gain) * (logistic * (1.0 + outgate * (1.0 - logistic)))
        ).astype(BF)
        gains_ref[...] += jnp.sum(grad_normed * unit, axis=0, keepdims=True)
        weighted = grad_normed * gain
        grad = (scale * (weighted - unit * jnp.mean(weighted * unit, axis=1, keepdims=True))).astype(BF)
        low = low_ref[rows, :]
        logit, running = gates(low, up_ref[...], bias_ref[...])
        middle = running[BLOCK // 2:BLOCK // 2 + 1, :]
        last = running[BLOCK - 1:BLOCK, :]
        rise, fall = jnp.exp(running - middle), jnp.exp(middle - running)
        enter, leave = jnp.exp(running), jnp.exp(last - running)
        query_wide = (query * rise).astype(BF)
        key_wide = (key * fall).astype(BF)
        query_in = (query * enter).astype(BF)
        key_out = (key * leave).astype(BF)
        before = states_ref[i, :, :]
        after = state[...]
        after_low = after.astype(BF)
        carried = transposed_times(value, key_out)
        ended = before.astype(F32) * jnp.exp(last) + carried
        boundary = jnp.sum(ended * after, axis=0, keepdims=True)
        scores = jnp.where(mask, times_transposed(query_wide, key_wide), 0.0).astype(BF)
        grad_scores = jnp.where(mask, times_transposed(grad, value), 0.0).astype(BF)
        grad_value = transposed_times(scores, grad) + times_transposed(key_out, after_low)
        query_term = matmul(grad_scores, key_wide) * rise + matmul(grad, before) * enter
        key_term = transposed_times(grad_scores, query_wide) * fall + matmul(value, after_low) * leave
        state[...] = after * jnp.exp(last) + transposed_times(grad, query_in)
        out_ref[rows, 0:kw] = (query_term * root).astype(BF)
        out_ref[rows, kw:2 * kw] = key_term.astype(BF)
        out_ref[rows, 2 * kw:2 * kw + vw] = grad_value.astype(BF)
        grad_decay = dot(suffix, query * query_term - key * key_term, 1, 0, HIGHEST) + boundary
        grad_logit = grad_decay * (sigmoid(-logit) / 16.0)
        sums_ref[...] += jnp.sum(grad_logit, axis=0, keepdims=True)
        upgrad_ref[...] += dot(low, grad_logit, 0, 0, HIGHEST)
        out_ref[rows, 2 * kw + 2 * vw:] = dot(grad_logit, wide_ref[...], 1, 1, HIGHEST).astype(BF)
        return 0

    lax.fori_loop(0, blocks, step, 0)


def vmem():
    return pl.BlockSpec(memory_space=pltpu.VMEM)


def mixer_forward(proj, lowrank, gate_up, gate_bias, gain):
    rows, (rank, kw), vw = proj.shape[0], gate_up.shape, gain.shape[1]
    blocks = rows // BLOCK
    return pl.pallas_call(
        functools.partial(forward_kernel, kw, vw),
        out_shape=(
            jax.ShapeDtypeStruct((rows, vw), BF),
            jax.ShapeDtypeStruct((rows, vw), BF),
            jax.ShapeDtypeStruct((blocks, vw, kw), BF),
        ),
        in_specs=[vmem()] * 5,
        out_specs=(vmem(),) * 3,
        scratch_shapes=[pltpu.VMEM((vw, kw), F32)],
        compiler_params=pltpu.CompilerParams(vmem_limit_bytes=40 * 2**20),
        cost_estimate=pl.CostEstimate(flops=20_000_000_000, bytes_accessed=10 * 2**20, transcendentals=0),
        name="mixer_forward",
    )(proj, lowrank, gate_up, gate_bias, gain)


def mixer_backward(proj, lowrank, gate_up, gate_bias, gain, mixed, states, grad):
    rows, (rank, kw), vw = proj.shape[0], gate_up.shape, gain.shape[1]
    wide = jnp.pad(gate_up, ((0, LANES - rank), (0, 0)))
    return pl.pallas_call(
        functools.partial(backward_kernel, kw, vw),
        out_shape=(
            jax.ShapeDtypeStruct((rows, proj.shape[1] + LANES), BF),
            jax.ShapeDtypeStruct((rank, kw), F32),
            jax.ShapeDtypeStruct((1, kw), F32),
            jax.ShapeDtypeStruct((1, vw), F32),
        ),
        in_specs=[vmem()] * 9,
        out_specs=(vmem(),) * 4,
        scratch_shapes=[pltpu.VMEM((vw, kw), F32)],
        compiler_params=pltpu.CompilerParams(vmem_limit_bytes=40 * 2**20),
        cost_estimate=pl.CostEstimate(flops=40_000_000_000, bytes_accessed=16 * 2**20, transcendentals=0),
        name="mixer_backward",
    )(proj, lowrank, gate_up, gate_bias, gain, mixed, states, grad, wide)


def swap(array, axis, bit):
    size = lax.axis_size(axis)
    return lax.ppermute(array, axis, [(i, i ^ bit) for i in range(size)])


def bits_of(size):
    return [1 << k for k in range(size.bit_length() - 1)]


def dp_bits():
    bits = bits_of(lax.axis_size("dp"))
    return bits[:1], bits[1:-1], bits[-1:]


def index_at(place):
    low, middle, top = dp_bits()
    return sum(bit for k, bit in enumerate([*middle, *top, *low]) if place >> k & 1)


def reorder(array, dim, back=False):
    me, size = lax.axis_index("dp"), lax.axis_size("dp")
    width = array.shape[dim] // size
    to = [0] * size
    for place in range(size):
        to[index_at(place)] = place
    places = []
    for p in range(size):
        if back:
            source = jnp.asarray(to, jnp.int32)[p ^ me]
        else:
            source = index_at(p) ^ me
        places.append(lax.dynamic_slice_in_dim(array, source * width, width, dim))
    return jnp.concatenate(places, dim)


class Flow:
    def __init__(self):
        self.fence, self.posted = (), []

    def send(self, array, axis, bit):
        got = swap(lax.optimization_barrier((array, self.fence))[0] if self.fence else array, axis, bit)
        self.posted.append(got)
        return got

    def note(self, *arrays):
        self.posted += arrays

    def turn(self):
        self.fence, self.posted = tuple(self.posted), []

    def held(self, array):
        return lax.optimization_barrier((array, self.fence))[0]


def after(array, *earlier):
    return lax.optimization_barrier((array, earlier))[0]


def pick(array, dim, count, places):
    width = array.shape[dim] // count
    return jnp.concatenate([lax.slice_in_dim(array, p * width, (p + 1) * width, axis=dim) for p in places], dim)


def grow(flow, array, bits, dim):
    for bit in bits:
        array = jnp.concatenate([array, flow.send(array, "dp", bit)], dim)
    return array


def turned(array, dim):
    count = lax.axis_size("dp") // 2
    return pick(array, dim, count, [*range(0, count, 2), *range(1, count, 2)])


def turned_back(array, dim):
    count = lax.axis_size("dp") // 2
    return pick(array, dim, count, [p for k in range(count // 2) for p in (k, count // 2 + k)])


def shrink(flow, array, bits, dim):
    for bit in bits:
        keep, give = jnp.split(array, 2, dim)
        array = keep + flow.send(give, "dp", bit)
    return array


def shrink_inner(flow, array, bits, dim):
    for bit in reversed(bits):
        keep = pick(array, dim, 4, [0, 2])
        give = pick(array, dim, 4, [1, 3])
        array = keep + flow.send(give, "dp", bit)
    return array


def gather_first(flow, one, two, dim):
    low, middle, top = dp_bits()
    return grow(flow, one, middle, dim), grow(flow, two, top, dim)


def gather_second(flow, one, two, dim):
    low, middle, top = dp_bits()
    return grow(flow, one, top, dim), turned(grow(flow, two, middle, dim), dim)


def gather_core(flow, one, two, dim):
    low, middle, top = dp_bits()
    return grow(flow, one, low, dim), grow(flow, two, low, dim)


def scatter_core(flow, one, two, dim):
    low, middle, top = dp_bits()
    return shrink(flow, one, low, dim), shrink(flow, two, low, dim)


def scatter_first(flow, one, two, dim):
    low, middle, top = dp_bits()
    return shrink(flow, one, top, dim), shrink_inner(flow, two, middle, dim)


def scatter_second(flow, one, two, dim):
    low, middle, top = dp_bits()
    return shrink(flow, one, middle[::-1], dim), shrink(flow, two, top, dim)


def gather_rows(array):
    return lax.all_gather(array, "tensor", axis=0, tiled=True)


def scatter_rows(array):
    return lax.psum_scatter(array, "tensor", scatter_dimension=0, tiled=True)


class Everywhere:
    def __init__(self, flow, array, axes):
        self.flow, self.array = flow, array
        bits = [[(axis, bit) for bit in bits_of(lax.axis_size(axis))] for axis in axes]
        self.left = [some[k] for k in range(max(map(len, bits))) for some in bits if k < len(some)]

    def step(self, count=1):
        for axis, bit in self.left[:count]:
            self.array = self.array + self.flow.send(self.array, axis, bit)
        self.left = self.left[count:]


def norm_scale(rows):
    return lax.rsqrt(jnp.mean(rows * rows, axis=1, keepdims=True) + EPS_NORM)


def norm_back(grad_normed, rows, scale, gain):
    weighted = grad_normed * gain
    return scale * weighted - rows * scale**3 * jnp.mean(weighted * rows, axis=1, keepdims=True)


def on_device(inputs, norm1_gain, query_weight, key_weight, value_weight, outgate_weight, gate_down,
              gate_up, gate_bias, group_gain, proj_weight, norm2_gain, ffn_gate, ffn_up, ffn_down, cotangent):
    head, heads = lax.axis_index("tensor"), lax.axis_size("tensor")
    own_rows = inputs.shape[0]
    units = ffn_gate.shape[1]
    kw, vw = query_weight.shape[1], value_weight.shape[1]
    inputs = reorder(inputs, 1)
    cotangent = reorder(cotangent, 1)
    gain_one = reorder(norm1_gain[None, :], 1)
    gain_two = reorder(norm2_gain[None, :], 1)
    gate_down = reorder(gate_down, 0)

    flow = Flow()
    inputs_wide = inputs.astype(F32)
    scale_one = norm_scale(inputs_wide)
    normed_one = (inputs_wide * scale_one * gain_one).astype(BF)

    shard_proj = gather_rows(proj_weight)
    rows_one = gather_rows(normed_one)
    into_shard = jnp.concatenate([query_weight, key_weight, value_weight, outgate_weight], 1)
    into = gather_first(flow, *jnp.split(into_shard, 2, 1), 0)
    flow.turn()
    into = gather_second(flow, *into, 0)
    flow.turn()
    into = gather_core(flow, *into, 0)
    flow.turn()
    proj_full = gather_first(flow, *jnp.split(shard_proj, 2, 0), 1)
    flow.turn()
    proj_full = gather_second(flow, *proj_full, 1)
    flow.turn()
    gate_up_full = gather_first(flow, ffn_gate, ffn_up, 0)
    proj_full = jnp.concatenate(gather_core(flow, *proj_full, 1), 0)
    flow.turn()
    cot_rows = gather_rows(after(cotangent, shard_proj)).reshape(heads, 2, own_rows // 2, -1)
    cot_rows = [cot_rows[:, k].reshape(heads * own_rows // 2, -1) for k in range(2)]

    down_wide = jnp.pad(gate_down, ((0, 0), (0, LANES - gate_down.shape[1])))
    into = jnp.concatenate([*into, down_wide], 1)
    projected = matmul(flow.held(rows_one), into[:, :2 * kw + 2 * vw]).astype(BF)
    lowrank = matmul(rows_one, gate_down)
    gate_row, gain_row = gate_bias[None, :], group_gain[None, :]
    gated, mixed, states = mixer_forward(projected, lowrank, gate_up, gate_row, gain_row)
    flow.note(gated)
    flow.turn()

    def exchange(pieces, dim):
        come = jnp.stack([pieces[0]] + [swap(pieces[m], "tensor", m) for m in range(1, heads)], 0)
        return jnp.concatenate(
            [lax.dynamic_index_in_dim(come, head ^ t, 0, keepdims=False) for t in range(heads)], dim
        )
    def rows_of(array, index):
        return lax.dynamic_slice_in_dim(array, index * own_rows, own_rows, 0)
    gated_own = exchange([rows_of(gated, head ^ m) for m in range(heads)], 1)
    gate_up_full = gather_second(flow, *gate_up_full, 0)
    flow.turn()
    resid = inputs_wide + lax.optimization_barrier(matmul(flow.held(after(gated_own, cot_rows)), proj_full))
    scale_two = norm_scale(resid)
    normed_two = (resid * scale_two * gain_two).astype(BF)
    rows_two = [gather_rows(part) for part in jnp.split(normed_two, 2, 0)]
    flow.note(normed_two)
    flow.turn()

    gate_full, up_full = gather_core(flow, *gate_up_full, 0)
    down_full = gather_first(flow, *jnp.split(ffn_down, 2, 0), 1)
    flow.turn()
    down_full = gather_second(flow, *down_full, 1)
    flow.turn()
    down_full = jnp.concatenate(gather_core(flow, *down_full, 1), 0)
    flow.turn()

    def feed_forward(rows, cot):
        gate_pre = matmul(rows, gate_full)
        up_pre = matmul(rows, up_full)
        logistic = sigmoid(gate_pre)
        act = gate_pre * logistic
        hidden = (act * up_pre).astype(BF)
        grad_hidden = times_transposed(cot, down_full)
        grad_up = (grad_hidden * act).astype(BF)
        grad_gate = (grad_hidden * up_pre * (logistic * (1.0 + gate_pre * (1.0 - logistic)))).astype(BF)
        back = (times_transposed(grad_gate, gate_full) + times_transposed(grad_up, up_full)).astype(BF)
        return hidden, grad_gate, grad_up, back
    first = feed_forward(rows_two[0], cot_rows[0])
    rows_two[1] = after(rows_two[1], first[3])
    hidden, grad_gate, grad_up, part_two = zip(first, feed_forward(rows_two[1], cot_rows[1]))

    grad_two = jnp.concatenate([scatter_rows(part) for part in part_two], 0).astype(F32)
    hidden, grad_gate, grad_up, rows_two, cot_rows = (
        jnp.concatenate(parts, 0) for parts in (hidden, grad_gate, grad_up, rows_two, cot_rows)
    )
    flow.note(part_two)
    flow.turn()
    gate_sums = transposed_times(rows_two, flow.held(grad_gate)).astype(BF)
    up_sums = transposed_times(rows_two, flow.held(grad_up)).astype(BF)
    gate_sums, up_sums = scatter_core(flow, gate_sums, up_sums, 0)
    flow.turn()
    gate_sums, up_sums = scatter_first(flow, gate_sums, up_sums, 0)
    down_sums = transposed_times(after(hidden, part_two), cot_rows).astype(BF)
    part_out = matmul(after(hidden, part_two), down_full).astype(BF)
    out_own = [scatter_rows(part) for part in jnp.split(part_out, 2, 0)]
    flow.note(part_out, down_sums)
    flow.turn()
    grad_two = flow.held(grad_two)
    norm2_term = jnp.sum(grad_two * resid * scale_two, axis=0, keepdims=True)
    grad_resid = cotangent.astype(F32) + norm_back(grad_two, resid, scale_two, gain_two)

    grad_branch = grad_resid.astype(BF)
    grad_gated_own = times_transposed(grad_branch, proj_full).astype(BF)
    flow.note(grad_gated_own)
    flow.turn()
    grad_gated = exchange(
        [lax.dynamic_slice_in_dim(grad_gated_own, (head ^ m) * vw, vw, 1) for m in range(heads)], 0
    )
    gate_sums, up_sums = scatter_second(flow, gate_sums, up_sums, 0)
    grad_gate_own, grad_up_own = gate_sums.astype(F32), up_sums.astype(F32)
    proj_sums = transposed_times(gated_own, flow.held(grad_branch)).astype(BF)
    proj_sums = scatter_core(flow, *jnp.split(proj_sums, 2, 0), 1)
    flow.turn()
    proj_sums = scatter_first(flow, *proj_sums, 1)

    grad_into, up_term, bias_term, group_term = mixer_backward(
        projected, lowrank, gate_up, gate_row, gain_row, mixed, states, flow.held(grad_gated)
    )
    grad_low = grad_into[:, 2 * kw + 2 * vw:2 * kw + 2 * vw + gate_down.shape[1]]
    flow.note(grad_into)
    flow.turn()
    output = (resid + jnp.concatenate(flow.held(out_own), 0).astype(F32)).astype(BF)
    total_low = times_transposed(grad_into, into).astype(BF)
    grad_one = scatter_rows(total_low).astype(F32)
    proj_sums = scatter_second(flow, *proj_sums, 1)
    flow.note(total_low)
    flow.turn()
    into_sums = transposed_times(rows_one, flow.held(grad_into)).astype(BF)
    into_sums = scatter_core(flow, *jnp.split(into_sums[:, :2 * kw + 2 * vw], 2, 1), 0)
    flow.turn()
    into_sums = scatter_first(flow, *into_sums, 0)
    norm1_term = jnp.sum(flow.held(total_low).astype(F32) * rows_one.astype(F32), axis=0, keepdims=True) / gain_one
    down_term = transposed_times(grad_low, rows_one)
    small = Everywhere(
        flow, reorder(jnp.concatenate([down_term, norm1_term, norm2_term], 0), 1, True), ("tensor", "dp")
    )
    by_head = Everywhere(
        flow, jnp.concatenate([up_term, bias_term, group_term[:, :kw], group_term[:, kw:]], 0), ("dp",)
    )
    by_head.step()
    flow.note(small.array)
    flow.turn()
    into_sums = scatter_second(flow, *into_sums, 0)
    small.step()
    by_head.step()
    flow.turn()
    down_sums = scatter_core(flow, *jnp.split(down_sums, 2, 0), 1)
    small.step()
    by_head.step(len(by_head.left))
    flow.turn()
    down_sums = scatter_first(flow, *down_sums, 1)
    small.step()
    flow.note(grad_one)
    flow.turn()
    proj_sums = jnp.concatenate(proj_sums, 0)
    grad_proj = lax.dynamic_slice_in_dim(proj_sums, head * vw, vw, 0).astype(F32)
    for m in range(1, heads):
        part = lax.dynamic_slice_in_dim(proj_sums, (head ^ m) * vw, vw, 0)
        grad_proj = grad_proj + swap(flow.held(part), "tensor", m).astype(F32)
    down_sums = scatter_second(flow, *down_sums, 1)
    small.step(len(small.left) - 1)
    flow.turn()
    small.step(len(small.left))
    grad_into_own = jnp.concatenate(into_sums, 1).astype(F32)
    grad_down_own = jnp.concatenate(down_sums, 0).astype(F32)
    grad_input = grad_resid + norm_back(grad_one, inputs_wide, scale_one, gain_one)
    summed, by_head = small.array, by_head.array
    rank = gate_down.shape[1]
    splits = [kw, 2 * kw, 2 * kw + vw]
    grad_query, grad_key, grad_value, grad_outgate = jnp.split(grad_into_own, splits, 1)
    return (
        reorder(output, 1, True),
        reorder(grad_input, 1, True),
        summed[rank],
        grad_query,
        grad_key,
        grad_value,
        grad_outgate,
        summed[:rank].T,
        by_head[:rank],
        by_head[rank],
        by_head[rank + 1:].reshape(-1),
        grad_proj,
        summed[rank + 1],
        grad_gate_own,
        grad_up_own,
        grad_down_own,
    )


def solution(mesh):
    tokens, whole = P(("dp", "tensor"), None), P()
    rows, columns = P("dp", "tensor"), P("tensor", "dp")
    last = P(None, "tensor")
    head = P("tensor")
    return jax.shard_map(
        on_device,
        mesh=mesh,
        in_specs=(tokens, whole, rows, rows, rows, rows, whole, last, head, head, columns, whole, rows, rows,
                  columns, tokens),
        out_specs=(tokens, tokens, whole, rows, rows, rows, rows, whole, last, head, head, columns, whole, rows,
                   rows, columns),
        check_vma=False,
    )
```
